1024 devices in a mesh: row: 16 (over z_hi, x), col: 8 (over y, core), layer: 8 (over z_lo).
Axes of the slice: x: 4, y: 4, z: 32 (z_hi: 4, z_lo: 8; z = z_hi * 8 + z_lo), core: 2. Of those that a mesh axis runs over, the one named last changes fastest.
Arguments:
- a_tiles: bfloat16 [8, 8192, 1024], P('layer', 'row', 'col'), may hold values from -0.25 to 0.25
- b_tiles: bfloat16 [8, 1024, 16384], P('layer', 'row', 'col'), may hold values from -6 to 6
- a_mask: int32 [8, 256, 32], P('layer', 'row', 'col'), may hold values from 0 to 1
- b_mask: int32 [8, 32, 512], P('layer', 'row', 'col'), may hold values from 0 to 1
- c_mask: int32 [256, 512], P('row', 'col'), may hold values from 0 to 1
Outputs:
- product: bfloat16 [8192, 16384], P(('row', 'layer'), 'col')
The draws below stay inside these ranges and needn't reach their ends.
All inputs are finite; a program needn't handle non-finite values.
Results may differ from the reference program's by a relative error of at most 0.001.
Values may be sent and summed in bfloat16 or wider, within the bound.
A program may use at most 64 MiB of HBM per device.

```python
import jax
import jax.numpy as jnp
from jax import lax

TILE = 32
K_TILES = 32
GROUPS = 8
KS = 1024
M = 8192
N = 16384


def banded_marks(key, rows_total, cols_total, inside, outside):
    row_ids = jnp.arange(rows_total, dtype=jnp.int32)[:, None]
    col_ids = jnp.arange(cols_total, dtype=jnp.int32)[None, :]
    center = row_ids * cols_total // rows_total
    offset = jnp.abs(center - col_ids)
    offset = jnp.minimum(offset, cols_total - offset)
    width_band = max(cols_total // 8, 1)
    limit = jnp.where(offset < width_band, inside, outside)
    rolls = jax.random.randint(key, (rows_total, cols_total), 0, 100)
    return (rolls < limit).astype(jnp.int32)


def draw_a_mask(key, part):
    key = jax.random.fold_in(key, 11)
    total_k = GROUPS * K_TILES
    marks = banded_marks(key, M // TILE, total_k, 70, 12)
    return marks.reshape(M // TILE, GROUPS, K_TILES).transpose(1, 0, 2)


def draw_b_mask(key, part):
    key = jax.random.fold_in(key, 23)
    total_k = GROUPS * K_TILES
    marks = banded_marks(key, N // TILE, total_k, 70, 12)
    return marks.T.reshape(GROUPS, K_TILES, N // TILE)


def draw_c_mask(key, part):
    key = jax.random.fold_in(key, 37)
    return banded_marks(key, M // TILE, N // TILE, 90, 15)


def block_levels(key, shape, pieces, least, high):
    factor_of, own = 1.0, jax.random.fold_in(key, 6)
    for axis_at, blocks in pieces:
        steps = jnp.exp(jax.random.uniform(jax.random.fold_in(own, axis_at), (blocks,), jnp.float32, least / len(pieces), high / len(pieces)))
        factor_of = factor_of * jnp.repeat(steps, shape[axis_at] // blocks).reshape([-1 if axis == axis_at else 1 for axis in range(len(shape))])
    return factor_of


def scatter_about(key, extent, deviation, bound, shards=(), held_as=jnp.bfloat16):
    drawn = deviation * jax.random.normal(key, extent, jnp.float32)
    if shards:
        drawn = drawn * block_levels(key, extent, shards, -0.22, 0.18)
    return jnp.clip(drawn, -bound, bound).astype(held_as)


def setup_inputs(seed: int = 0) -> dict:
    streams_of = jax.random.split(jax.random.key(seed), 6)
    a_tiles = scatter_about(streams_of[0], (GROUPS, M, KS), (GROUPS * KS // 16) ** -0.5, 0.25, ((0, 8), (1, 16), (2, 8)))
    b_tiles = scatter_about(streams_of[1], (GROUPS, KS, N), 1.0, 6.0, ((0, 8), (1, 16), (2, 8)))
    a_mask = draw_a_mask(jax.random.fold_in(streams_of[5], 71), 0)
    b_mask = draw_b_mask(jax.random.fold_in(streams_of[5], 71), 0)
    c_mask = draw_c_mask(jax.random.fold_in(streams_of[5], 71), 0)
    return {"a_tiles": a_tiles, "b_tiles": b_tiles, "a_mask": a_mask, "b_mask": b_mask, "c_mask": c_mask}


def expand_tiles(values, marks):
    height, width = values.shape
    factor = marks.astype(values.dtype)
    blocks = values.reshape(height // TILE, TILE, width // TILE, TILE) * factor[:, None, :, None]
    return blocks.reshape(height, width)


def reference(a_tiles, b_tiles, a_mask, b_mask, c_mask):
    def add_group(group_index, running):
        left_side = expand_tiles(a_tiles[group_index], a_mask[group_index])
        right_side = expand_tiles(b_tiles[group_index], b_mask[group_index])
        return running + jnp.dot(left_side, right_side, preferred_element_type=jnp.float32)

    summed = lax.fori_loop(0, GROUPS, add_group, jnp.zeros((M, N), jnp.float32))
    return expand_tiles(summed, c_mask).astype(jnp.bfloat16)
```

```python
import jax
import jax.numpy as jnp
from jax import lax
from jax.experimental import pallas as pl
from jax.experimental.pallas import tpu as pltpu
from jax.sharding import PartitionSpec as P

TILE = 32
RUN = 8
RING = 32
SIDE = 4
WIDE = 256
DEEP = 64
ROWS = 512
NARROW = 128
MESH = pl.DeviceIdType.MESH
F32 = jnp.float32
BF16 = jnp.bfloat16


def device(x, y, z, core):
    return ((z // RUN) * SIDE + x, y * 2 + core, z % RUN)


def piece_of(z):
    low = z % RUN
    return jnp.where((z // RUN) % 2 == 0, low, RUN - 1 - low)


def frame_of(source, piece):
    m = jnp.where(piece < RUN // 2, piece, RUN - 1 - piece)
    turn = jnp.where(piece < RUN // 2, 0, RUN)
    ahead = lax.rem(source - turn - m + 2 * RING, RING)
    start = lax.rem(turn + 16 * (ahead // 16), RING)
    return m, start, m + lax.rem(ahead, 16)


def spread_rows(factor):
    height, width = factor.shape
    return jnp.broadcast_to(factor[:, None, :], (height, TILE, width)).reshape(height * TILE, width)


def kernel(
    a_ref, b_ref, a_mask_ref, b_mask_ref, c_mask_ref, o_ref,
    left, right, own, total, done, landed,
    b_send, b_pass, b_recv, x_send, x_recv, a_send, a_recv, y_send, y_recv, k_send, k_recv, c_send, c_recv,
):
    row, col, zl = lax.axis_index("row"), lax.axis_index("col"), lax.axis_index("layer")
    x, zh = lax.rem(row, SIDE), row // SIDE
    y, core = col // 2, lax.rem(col, 2)
    z = zh * RUN + zl
    mine = piece_of(z)

    def at_z(there):
        return device(x, y, lax.rem(there + RING, RING), core)

    def at_x(step):
        return device(lax.rem(x + step, SIDE), y, z, core)

    def at_y(step):
        return device(x, lax.rem(y + step, SIDE), z, core)

    other = device(x, y, z, 1 - core)

    barrier = pltpu.get_barrier_semaphore()

    @pl.loop(1, RING)
    def _(step):
        pl.semaphore_signal(barrier, inc=1, device_id=at_z(z + step), device_id_type=MESH)

    for step in range(1, SIDE):
        pl.semaphore_signal(barrier, inc=1, device_id=at_x(step), device_id_type=MESH)
        pl.semaphore_signal(barrier, inc=1, device_id=at_y(step), device_id_type=MESH)
    pl.semaphore_signal(barrier, inc=1, device_id=other, device_id_type=MESH)

    marks = a_mask_ref[...].astype(F32)
    lane = lax.broadcasted_iota(jnp.int32, (ROWS // TILE, NARROW), 1) // TILE
    factor = jnp.zeros((ROWS // TILE, NARROW), F32)
    for tile in range(NARROW // TILE):
        factor = jnp.where(lane == tile, marks[:, tile : tile + 1], factor)
    left[zl, core, y] = (a_ref[...].astype(F32) * spread_rows(factor)).astype(BF16)

    width = b_ref.shape[1]
    tiles = width // TILE
    marks = b_mask_ref[...].astype(F32)
    spread = (
        lax.broadcasted_iota(jnp.int32, (tiles, width), 0) == lax.broadcasted_iota(jnp.int32, (tiles, width), 1) // TILE
    ).astype(F32)
    factor = spread_rows(jnp.dot(marks, spread, preferred_element_type=F32))
    for piece in range(RUN):
        cut = slice(piece * WIDE, (piece + 1) * WIDE)
        own[piece] = (b_ref[:, cut].astype(F32) * factor[:, cut]).astype(BF16)
    right[zl, zh, x] = own[mine]

    pl.semaphore_wait(barrier, RING - 1 + 2 * (SIDE - 1) + 1)

    def a_hop(low, to):
        return pltpu.make_async_remote_copy(
            src_ref=left.at[low, core, y], dst_ref=left.at[low, core, y],
            send_sem=a_send.at[low, jnp.where(to > zl, 1, 0)], recv_sem=a_recv.at[low],
            device_id=device(x, y, zh * RUN + to, core), device_id_type=MESH,
        )

    def a_side(low, step):
        return pltpu.make_async_remote_copy(
            src_ref=left.at[low, core, y], dst_ref=left.at[low, core, y],
            send_sem=y_send.at[low, step - 1], recv_sem=y_recv.at[low],
            device_id=at_y(step), device_id_type=MESH,
        )

    def a_core(low):
        return pltpu.make_async_remote_copy(
            src_ref=left.at[low, core], dst_ref=left.at[low, core],
            send_sem=k_send.at[low], recv_sem=k_recv.at[low],
            device_id=other, device_id_type=MESH,
        )

    def a_onward(low):
        @pl.when((low <= zl) & (zl < RUN - 1))
        def _():
            a_hop(low, zl + 1).start()

        @pl.when((low >= zl) & (zl > 0))
        def _():
            a_hop(low, zl - 1).start()

        for step in (1, 3, 2):
            a_side(low, step).start()

    def a_arrive(low):
        pltpu.make_async_copy(left.at[low, core, y], left.at[low, core, y], a_recv.at[low]).wait()
        a_onward(low)

    def a_share(low):
        view = left.at[low, core, pl.ds(0, SIDE - 1)]
        pltpu.make_async_copy(view, view, y_recv.at[low]).wait()
        a_core(low).start()

    def both_ways(step, act):
        @pl.when(zl - step >= 0)
        def _():
            act(zl - step)

        @pl.when(zl + step < RUN)
        def _():
            act(zl + step)

    def b_first(piece, to, way):
        return pltpu.make_async_remote_copy(
            src_ref=own.at[piece], dst_ref=right.at[zl, zh, x],
            send_sem=b_send.at[piece, way], recv_sem=b_recv.at[z],
            device_id=at_z(to), device_id_type=MESH,
        )

    def b_next(source, to):
        low, high = lax.rem(source, RUN), source // RUN
        return pltpu.make_async_remote_copy(
            src_ref=right.at[low, high, x], dst_ref=right.at[low, high, x],
            send_sem=b_pass.at[source], recv_sem=b_recv.at[source],
            device_id=at_z(to), device_id_type=MESH,
        )

    def b_side(source, step):
        low, high = lax.rem(source, RUN), source // RUN
        return pltpu.make_async_remote_copy(
            src_ref=right.at[low, high, x], dst_ref=right.at[low, high, x],
            send_sem=x_send.at[source, step - 1], recv_sem=x_recv.at[source],
            device_id=at_x(step), device_id_type=MESH,
        )

    def first_of(piece):
        m, start, at = frame_of(z, piece)
        inside = at <= 15 - m
        up = jnp.where(inside, 15 - m, 16 + m)
        down = jnp.where(inside, m, 15 - m)
        return lax.rem(start + up, RING), at != up, lax.rem(start + down, RING), at != down

    def route(source):
        m, start, at = frame_of(source, mine)
        here = lax.rem(z - start + RING, RING)
        inside = at <= 15 - m
        odd = lax.rem(source + mine, 2) == 1
        t0, t1, t2, t3 = m, 15 - m, 16 + m, 31 - m
        is0, is1, is2, is3 = here == t0, here == t1, here == t2, here == t3
        hops_in = jnp.where(is0 | is1, 1, 2)
        to_in = jnp.where(is0, t3, jnp.where(is1, t2, -1))
        hops_up = jnp.where(is1 | is2, 1, jnp.where(is3, 2, 3))
        to_up = jnp.where(is2, t3, jnp.where(is3, t0, -1))
        hops_down = jnp.where(is1 | is2, 1, jnp.where(is0, 2, 3))
        to_down = jnp.where(is1, t0, jnp.where(is0, t3, -1))
        hops = jnp.where(inside, hops_in, jnp.where(odd, hops_up, hops_down))
        to = jnp.where(inside, to_in, jnp.where(odd, to_up, to_down))
        return hops, to >= 0, lax.rem(start + to + RING, RING)

    def b_handle(source, hops_now):
        hops, onward, to = route(source)

        @pl.when(hops == hops_now)
        def _():
            low, high = lax.rem(source, RUN), source // RUN

            @pl.when(source != z)
            def _():
                pltpu.make_async_copy(right.at[low, high, x], right.at[low, high, x], b_recv.at[source]).wait()

            @pl.when(onward)
            def _():
                b_next(source, to).start()

            for step in (1, 3, 2):
                b_side(source, step).start()

    def source_at(index):
        away = (index + 1) // 2
        return lax.rem(z + jnp.where(lax.rem(index, 2) == 0, away, RING - away), RING)

    a_onward(zl)

    @pl.loop(0, RUN)
    def _(step):
        piece = lax.rem(mine + step, RUN)
        to_up, up, to_down, down = first_of(piece)

        @pl.when(up)
        def _():
            b_first(piece, to_up, 1).start()

        @pl.when(down)
        def _():
            b_first(piece, to_down, 0).start()

    @pl.loop(0, RUN)
    def _(step):
        @pl.loop(0, RING // RUN)
        def _(index):
            b_handle(source_at(step * (RING // RUN) + index), 1)

        both_ways(step + 1, a_arrive)

    a_share(zl)

    @pl.loop(0, RUN)
    def _(step):
        @pl.loop(0, RING // RUN)
        def _(index):
            b_handle(source_at(step * (RING // RUN) + index), 2)

        both_ways(step + 1, a_share)

    @pl.loop(0, RING)
    def _(index):
        b_handle(source_at(index), 3)

    total[...] = jnp.zeros_like(total)

    @pl.loop(0, RUN)
    def _(low):
        pltpu.make_async_copy(left.at[low, core], left.at[low, core], k_recv.at[low]).wait()
        for high in range(RING // RUN):
            view = right.at[low, high, pl.ds(0, SIDE - 1)]
            pltpu.make_async_copy(view, view, x_recv.at[high * RUN + low]).wait()
        blocks = [left[low, c, s] for s in range(SIDE) for c in range(2)]
        total[...] += jnp.dot(
            jnp.concatenate(blocks, axis=1),
            right[low].reshape(RING // RUN * SIDE * DEEP, WIDE),
            preferred_element_type=F32,
        )

    keep = (
        lax.broadcasted_iota(jnp.int32, (tiles, WIDE), 0)
        == lax.broadcasted_iota(jnp.int32, (tiles, WIDE), 1) // TILE + mine * (WIDE // TILE)
    ).astype(F32)
    factor = jnp.dot(c_mask_ref[...].astype(F32), keep, preferred_element_type=F32)
    done[...] = (total[...] * spread_rows(factor)).astype(BF16).reshape(RUN, ROWS // RUN, WIDE)
    landed[mine] = done[zl]

    def c_out(low):
        return pltpu.make_async_remote_copy(
            src_ref=done.at[low], dst_ref=landed.at[mine],
            send_sem=c_send.at[low], recv_sem=c_recv,
            device_id=device(x, y, zh * RUN + low, core), device_id_type=MESH,
        )

    @pl.loop(1, RUN)
    def _(step):
        c_out(lax.rem(zl + step, RUN)).start()

    view = landed.at[pl.ds(0, RUN - 1)]
    pltpu.make_async_copy(view, view, c_recv).wait()
    for piece in range(RUN):
        o_ref[:, piece * WIDE : (piece + 1) * WIDE] = landed[piece]

    @pl.loop(0, RUN)
    def _(index):
        @pl.when((index <= zl) & (zl < RUN - 1))
        def _():
            a_hop(index, zl + 1).wait_send()

        @pl.when((index >= zl) & (zl > 0))
        def _():
            a_hop(index, zl - 1).wait_send()

        for step in (1, 2, 3):
            a_side(index, step).wait_send()
        a_core(index).wait_send()

        to_up, up, to_down, down = first_of(index)

        @pl.when(up)
        def _():
            b_first(index, to_up, 1).wait_send()

        @pl.when(down)
        def _():
            b_first(index, to_down, 0).wait_send()

        @pl.when(index != zl)
        def _():
            c_out(index).wait_send()

    @pl.loop(0, RING)
    def _(source):
        _, onward, to = route(source)

        @pl.when(onward)
        def _():
            b_next(source, to).wait_send()

        for step in (1, 2, 3):
            b_side(source, step).wait_send()


def body(a_tiles, b_tiles, a_mask, b_mask, c_mask):
    width = b_tiles.shape[2]
    dma = pltpu.SemaphoreType.DMA
    return pl.pallas_call(
        kernel,
        out_shape=jax.ShapeDtypeStruct((ROWS // RUN, width), BF16),
        in_specs=[pl.BlockSpec(memory_space=pltpu.VMEM)] * 5,
        out_specs=pl.BlockSpec(memory_space=pltpu.VMEM),
        scratch_shapes=[
            pltpu.VMEM((RUN, 2, SIDE, ROWS, NARROW), BF16),
            pltpu.VMEM((RUN, RING // RUN, SIDE, DEEP, WIDE), BF16),
            pltpu.VMEM((RUN, DEEP, WIDE), BF16),
            pltpu.VMEM((ROWS, WIDE), F32),
            pltpu.VMEM((RUN, ROWS // RUN, WIDE), BF16),
            pltpu.VMEM((RUN, ROWS // RUN, WIDE), BF16),
            dma((RUN, 2)), dma((RING,)), dma((RING,)),
            dma((RING, SIDE - 1)), dma((RING,)),
            dma((RUN, 2)), dma((RUN,)),
            dma((RUN, SIDE - 1)), dma((RUN,)),
            dma((RUN,)), dma((RUN,)),
            dma((RUN,)), dma,
        ],
        compiler_params=pltpu.CompilerParams(
            collective_id=0, has_side_effects=True, vmem_limit_bytes=40 << 20
        ),
        cost_estimate=pl.CostEstimate(
            flops=2 * ROWS * WIDE * 8192, bytes_accessed=1 << 20, transcendentals=0
        ),
        name="purify",
    )(a_tiles[0], b_tiles[0], a_mask[0], b_mask[0], c_mask)


def solution(mesh):
    placed = (
        P("layer", "row", "col"),
        P("layer", "row", "col"),
        P("layer", "row", "col"),
        P("layer", "row", "col"),
        P("row", "col"),
    )
    return jax.shard_map(
        body, mesh=mesh, in_specs=placed, out_specs=P(("row", "layer"), "col"), check_vma=False
    )
```

```python
import jax
import jax.numpy as jnp
from jax import lax
from jax.experimental import pallas as pl
from jax.experimental.pallas import tpu as pltpu
from jax.sharding import PartitionSpec as P

TILE = 32
RUN = 8
RING = 32
SIDE = 4
WIDE = 256
DEEP = 64
ROWS = 512
NARROW = 128
HALVES = 1
HALF = WIDE // HALVES
GPS = 2
LAG2 = 3
LAG3 = 4
MESH = pl.DeviceIdType.MESH
F32 = jnp.float32
BF16 = jnp.bfloat16


def device(x, y, z, core):
    return (lax.div(z, RUN) * SIDE + x, y * 2 + core, lax.rem(z, RUN))


def wrap(number, size):
    return jnp.where(number >= size, number - size, number)


def mirrored(index, high):
    return jnp.where(high % 2 == 0, index, RUN - 1 - index)


def lap_of(source, piece):
    early = piece < RUN // 2
    m = jnp.where(early, piece, RUN - 1 - piece)
    ahead = source - jnp.where(early, m, m + RUN)
    ahead = jnp.where(ahead < 0, ahead + RING, ahead)
    far = ahead >= 16
    return 15 - 2 * m, jnp.where(far, ahead - 16, ahead), far


def spread_rows(factor):
    height, width = factor.shape
    return jnp.broadcast_to(factor[:, None, :], (height, TILE, width)).reshape(height * TILE, width)


def kernel(
    a_ref, b_ref, a_mask_ref, b_mask_ref, c_mask_ref, o_ref,
    a_in, b_in, left, right, own, total, done, landed,
    in_sem, b_send, b_pass, b_recv, x_send, x_recv, a_send, a_recv, y_send, y_recv, k_send, k_recv, c_send, c_recv,
):
    row, col, zl = lax.axis_index("row"), lax.axis_index("col"), lax.axis_index("layer")
    x, zh = lax.rem(row, SIDE), row // SIDE
    y, core = col // 2, lax.rem(col, 2)
    z = zh * RUN + zl
    mine = mirrored(zl, zh)

    a_copy = pltpu.make_async_copy(a_ref, a_in, in_sem.at[0])
    b_copy = pltpu.make_async_copy(b_ref, b_in, in_sem.at[1])
    a_copy.start()
    b_copy.start()

    def at_z(there):
        return device(x, y, there, core)

    def at_x(step):
        return device(wrap(x + step, SIDE), y, z, core)

    def at_y(step):
        return device(x, wrap(y + step, SIDE), z, core)

    other = device(x, y, z, 1 - core)

    barrier = pltpu.get_barrier_semaphore()

    for high in range(RING // RUN):
        for low in range(RUN):
            @pl.when((zl != low) | (zh != high))
            def _():
                pl.semaphore_signal(barrier, inc=1, device_id=(high * SIDE + x, col, low), device_id_type=MESH)

    for step in range(1, SIDE):
        pl.semaphore_signal(barrier, inc=1, device_id=at_x(step), device_id_type=MESH)
        pl.semaphore_signal(barrier, inc=1, device_id=at_y(step), device_id_type=MESH)
    pl.semaphore_signal(barrier, inc=1, device_id=other, device_id_type=MESH)

    marks = a_mask_ref[...].astype(F32)
    lane = lax.broadcasted_iota(jnp.int32, (ROWS // TILE, NARROW), 1) // TILE
    factor = jnp.zeros((ROWS // TILE, NARROW), F32)
    for tile in range(NARROW // TILE):
        factor = jnp.where(lane == tile, marks[:, tile : tile + 1], factor)
    a_copy.wait()
    left[zl, core, y] = (a_in[...].astype(F32) * spread_rows(factor)).astype(BF16)

    width = b_ref.shape[1]
    tiles = width // TILE
    marks = b_mask_ref[...].astype(F32)
    spread = (
        lax.broadcasted_iota(jnp.int32, (tiles, width), 0) == lax.broadcasted_iota(jnp.int32, (tiles, width), 1) // TILE
    ).astype(F32)
    factor = spread_rows(jnp.dot(marks, spread, preferred_element_type=F32))
    b_copy.wait()
    for piece in range(RUN):
        for half in range(HALVES):
            cut = slice(piece * WIDE + half * HALF, piece * WIDE + (half + 1) * HALF)
            own[half, piece] = (b_in[:, cut].astype(F32) * factor[:, cut]).astype(BF16)
    for half in range(HALVES):
        right[half, mine, x, zh] = own[half, mine]

    pl.semaphore_wait(barrier, RING - 1 + 2 * (SIDE - 1) + 1)

    def a_hop(low, to):
        return pltpu.make_async_remote_copy(
            src_ref=left.at[low, core, y], dst_ref=left.at[low, core, y],
            send_sem=a_send.at[low, jnp.where(to > zl, 1, 0)], recv_sem=a_recv.at[low],
            device_id=device(x, y, zh * RUN + to, core), device_id_type=MESH,
        )

    def a_side(low, step):
        return pltpu.make_async_remote_copy(
            src_ref=left.at[low, core, y], dst_ref=left.at[low, core, y],
            send_sem=y_send.at[low, step - 1], recv_sem=y_recv.at[low],
            device_id=at_y(step), device_id_type=MESH,
        )

    def a_core(low):
        return pltpu.make_async_remote_copy(
            src_ref=left.at[low, core], dst_ref=left.at[low, core],
            send_sem=k_send.at[low], recv_sem=k_recv.at[low],
            device_id=other, device_id_type=MESH,
        )

    def a_onward(low):
        @pl.when((low <= zl) & (zl < RUN - 1))
        def _():
            a_hop(low, zl + 1).start()

        @pl.when((low >= zl) & (zl > 0))
        def _():
            a_hop(low, zl - 1).start()

        for step in (1, 3, 2):
            a_side(low, step).start()

    def a_arrive(low):
        pltpu.make_async_copy(left.at[low, core, y], left.at[low, core, y], a_recv.at[low]).wait()
        a_onward(low)

    def a_share(low):
        view = left.at[low, core, pl.ds(0, SIDE - 1)]
        pltpu.make_async_copy(view, view, y_recv.at[low]).wait()
        a_core(low).start()

    def both_ways(step, act):
        @pl.when(zl - step >= 0)
        def _():
            act(zl - step)

        @pl.when(zl + step < RUN)
        def _():
            act(zl + step)

    def b_first(half, piece, to, way):
        return pltpu.make_async_remote_copy(
            src_ref=own.at[half, piece], dst_ref=right.at[half, mine, x, zh],
            send_sem=b_send.at[half, piece, way], recv_sem=b_recv.at[half, mine, zh],
            device_id=at_z(to), device_id_type=MESH,
        )

    def b_next(half, index, high, to):
        return pltpu.make_async_remote_copy(
            src_ref=right.at[half, index, x, high], dst_ref=right.at[half, index, x, high],
            send_sem=b_pass.at[half, index, high], recv_sem=b_recv.at[half, index, high],
            device_id=at_z(to), device_id_type=MESH,
        )

    def b_side(half, index, high, step):
        return pltpu.make_async_remote_copy(
            src_ref=right.at[half, index, x, high], dst_ref=right.at[half, index, x, high],
            send_sem=x_send.at[half, index, high, step - 1], recv_sem=x_recv.at[half, index],
            device_id=at_x(step), device_id_type=MESH,
        )

    def first_of(piece):
        gap, behind, _ = lap_of(z, piece)
        inside = behind <= gap
        up = jnp.where(inside, gap, 16) - behind
        down = behind - jnp.where(inside, 0, gap)
        return wrap(z + up, RING), up > 0, wrap(z - down + RING, RING), down > 0

    wide, behind_me, far_me = lap_of(z, mine)
    role = jnp.where(behind_me == 0, 0, 1) + jnp.where(far_me, 2, 0)
    narrow = 16 - wide

    def part(role):
        inside = jnp.where(role < 2, 1, 2), jnp.where(role == 0, -narrow, jnp.where(role == 1, narrow, 0))
        middle = (role == 1) | (role == 2)
        odd = (
            jnp.where(middle, 1, jnp.where(role == 3, 2, 3)),
            jnp.where(role == 2, wide, jnp.where(role == 3, narrow, 0)),
        )
        even = (
            jnp.where(middle, 1, jnp.where(role == 0, 2, 3)),
            jnp.where(role == 1, -wide, jnp.where(role == 0, -narrow, 0)),
        )
        return [64 * hops + 32 + step for hops, step in (inside, odd, even)]

    near_parts = part(role)
    far_parts = part(wrap(role + 2, 4))

    def route(index, high):
        low = mirrored(index, high)
        _, behind, far = lap_of(high * RUN + low, mine)
        near_code = jnp.where(behind <= wide, near_parts[0], jnp.where(lax.rem(low + mine, 2) == 1, near_parts[1], near_parts[2]))
        far_code = jnp.where(behind <= wide, far_parts[0], jnp.where(lax.rem(low + mine, 2) == 1, far_parts[1], far_parts[2]))
        code = jnp.where(far, far_code, near_code)
        step = lax.rem(code, 64) - 32
        return lax.div(code, 64), step != 0, lax.rem(z + step + RING, RING)

    def group_of(stage):
        half = stage // RUN
        return half, wrap(mine - (stage - half * RUN) + RUN, RUN)

    def b_launch(stage):
        half = stage // RUN
        piece = wrap(mine + stage - half * RUN, RUN)
        to_up, up, to_down, down = first_of(piece)

        @pl.when(up)
        def _():
            b_first(half, piece, to_up, 1).start()

        @pl.when(down)
        def _():
            b_first(half, piece, to_down, 0).start()

    def b_handle(stage, hops_now):
        half, index = group_of(stage)
        for high in range(RING // RUN):
            hops, onward, to = route(index, high)

            @pl.when(hops == hops_now)
            def _():
                @pl.when((index != mine) | (high != zh))
                def _():
                    view = right.at[half, index, x, high]
                    pltpu.make_async_copy(view, view, b_recv.at[half, index, high]).wait()

                @pl.when(onward)
                def _():
                    b_next(half, index, high, to).start()

                for side in (1, 3, 2):
                    b_side(half, index, high, side).start()

    def use(stage):
        half, index = group_of(stage)
        view = right.at[half, index, pl.ds(0, SIDE - 1)]
        pltpu.make_async_copy(view, view, x_recv.at[half, index]).wait()
        lows = [index if high % 2 == 0 else RUN - 1 - index for high in range(RING // RUN)]
        blocks = [left[lows[high], c, high] for high in range(SIDE) for c in range(2)]
        depths = [right[half, index, s, high] for high in range(RING // RUN) for s in range(SIDE)]
        total[half] += jnp.dot(
            jnp.concatenate(blocks, axis=1), jnp.concatenate(depths, axis=0), preferred_element_type=F32
        )

    def c_out(half, low):
        return pltpu.make_async_remote_copy(
            src_ref=done.at[half, low], dst_ref=landed.at[half, mine],
            send_sem=c_send.at[half, low], recv_sem=c_recv.at[half],
            device_id=device(x, y, zh * RUN + low, core), device_id_type=MESH,
        )

    def finish(half):
        keep = (
            lax.broadcasted_iota(jnp.int32, (tiles, HALF), 0)
            == lax.broadcasted_iota(jnp.int32, (tiles, HALF), 1) // TILE + mine * (WIDE // TILE) + half * (HALF // TILE)
        ).astype(F32)
        factor = jnp.dot(c_mask_ref[...].astype(F32), keep, preferred_element_type=F32)
        done[half] = (total[half] * spread_rows(factor)).astype(BF16).reshape(RUN, ROWS // RUN, HALF)

        @pl.loop(1, RUN)
        def _(step):
            c_out(half, wrap(zl + step, RUN)).start()

        landed[half, mine] = done[half, zl]

    a_onward(zl)
    total[...] = jnp.zeros_like(total)

    @pl.loop(0, RUN)
    def _(stage):
        b_launch(stage)

    last = max(RUN + 1, RUN // GPS + LAG3)

    def staged(step, act):
        for turn in range(GPS):
            stage = step * GPS + turn

            @pl.when((stage >= 0) & (stage < RUN))
            def _():
                act(stage)

    @pl.loop(0, last)
    def _(step):
        @pl.when(step < RUN - 1)
        def _():
            both_ways(step + 1, a_arrive)

        staged(step, lambda stage: b_handle(stage, 1))
        staged(step - LAG2, lambda stage: b_handle(stage, 2))
        staged(step - LAG3, lambda stage: b_handle(stage, 3))

        @pl.when((step >= 1) & (step < RUN + 1))
        def _():
            @pl.when(step == 1)
            def _():
                a_share(zl)

            @pl.when(step > 1)
            def _():
                both_ways(step - 1, a_share)

    @pl.loop(0, RUN)
    def _(low):
        pltpu.make_async_copy(left.at[low, core], left.at[low, core], k_recv.at[low]).wait()

    @pl.loop(0, RUN)
    def _(stage):
        use(stage)

    finish(HALVES - 1)

    @pl.loop(0, RUN)
    def _(index):
        @pl.when((index <= zl) & (zl < RUN - 1))
        def _():
            a_hop(index, zl + 1).wait_send()

        @pl.when((index >= zl) & (zl > 0))
        def _():
            a_hop(index, zl - 1).wait_send()

        for step in (1, 2, 3):
            a_side(index, step).wait_send()
        a_core(index).wait_send()

        to_up, up, to_down, down = first_of(index)
        for half in range(HALVES):
            @pl.when(up)
            def _():
                b_first(half, index, to_up, 1).wait_send()

            @pl.when(down)
            def _():
                b_first(half, index, to_down, 0).wait_send()

            for high in range(RING // RUN):
                for step in (1, 2, 3):
                    b_side(half, index, high, step).wait_send()

        for high in range(RING // RUN):
            _, onward, to = route(index, high)

            @pl.when(onward)
            def _():
                for half in range(HALVES):
                    b_next(half, index, high, to).wait_send()

    for half in range(HALVES):
        view = landed.at[half, pl.ds(0, RUN - 1)]
        pltpu.make_async_copy(view, view, c_recv.at[half]).wait()
        for piece in range(RUN):
            cut = slice(piece * WIDE + half * HALF, piece * WIDE + (half + 1) * HALF)
            o_ref[:, cut] = landed[half, piece]

    @pl.loop(0, RUN)
    def _(index):
        @pl.when(index != zl)
        def _():
            for half in range(HALVES):
                c_out(half, index).wait_send()


def body(a_tiles, b_tiles, a_mask, b_mask, c_mask):
    width = b_tiles.shape[2]
    dma = pltpu.SemaphoreType.DMA
    runs = RING // RUN
    return pl.pallas_call(
        kernel,
        out_shape=jax.ShapeDtypeStruct((ROWS // RUN, width), BF16),
        in_specs=[pl.BlockSpec(memory_space=pltpu.HBM)] * 2 + [pl.BlockSpec(memory_space=pltpu.VMEM)] * 3,
        out_specs=pl.BlockSpec(memory_space=pltpu.VMEM),
        scratch_shapes=[
            pltpu.VMEM((ROWS, NARROW), BF16),
            pltpu.VMEM((DEEP, width), BF16),
            pltpu.VMEM((RUN, 2, SIDE, ROWS, NARROW), BF16),
            pltpu.VMEM((HALVES, RUN, SIDE, runs, DEEP, HALF), BF16),
            pltpu.VMEM((HALVES, RUN, DEEP, HALF), BF16),
            pltpu.VMEM((HALVES, ROWS, HALF), F32),
            pltpu.VMEM((HALVES, RUN, ROWS // RUN, HALF), BF16),
            pltpu.VMEM((HALVES, RUN, ROWS // RUN, HALF), BF16),
            dma((2,)),
            dma((HALVES, RUN, 2)), dma((HALVES, RUN, runs)), dma((HALVES, RUN, runs)),
            dma((HALVES, RUN, runs, SIDE - 1)), dma((HALVES, RUN)),
            dma((RUN, 2)), dma((RUN,)),
            dma((RUN, SIDE - 1)), dma((RUN,)),
            dma((RUN,)), dma((RUN,)),
            dma((HALVES, RUN)), dma((HALVES,)),
        ],
        compiler_params=pltpu.CompilerParams(
            collective_id=0, has_side_effects=True, vmem_limit_bytes=63 << 20
        ),
        cost_estimate=pl.CostEstimate(
            flops=2 * ROWS * WIDE * 8192, bytes_accessed=1 << 20, transcendentals=0
        ),
        name="purify",
    )(a_tiles[0], b_tiles[0], a_mask[0], b_mask[0], c_mask)


def solution(mesh):
    placed = (
        P("layer", "row", "col"),
        P("layer", "row", "col"),
        P("layer", "row", "col"),
        P("layer", "row", "col"),
        P("row", "col"),
    )
    return jax.shard_map(
        body, mesh=mesh, in_specs=placed, out_specs=P(("row", "layer"), "col"), check_vma=False
    )
```

```python
import jax
import jax.numpy as jnp
from jax import lax
from jax.experimental import pallas as pl
from jax.experimental.pallas import tpu as pltpu
from jax.sharding import PartitionSpec as P

TILE = 32
RUN = 8
RING = 32
SIDE = 4
WIDE = 256
DEEP = 64
ROWS = 512
NARROW = 128
HALVES = 1
HALF = WIDE // HALVES
GPS = 2
LAG2 = 3
LAG3 = 4
MESH = pl.DeviceIdType.MESH
F32 = jnp.float32
BF16 = jnp.bfloat16


def device(x, y, z, core):
    return (lax.div(z, RUN) * SIDE + x, y * 2 + core, lax.rem(z, RUN))


def wrap(number, size):
    return jnp.where(number >= size, number - size, number)


def mirrored(index, high):
    return jnp.where(high % 2 == 0, index, RUN - 1 - index)


def lap_of(source, piece):
    early = piece < RUN // 2
    m = jnp.where(early, piece, RUN - 1 - piece)
    ahead = source - jnp.where(early, m, m + RUN)
    ahead = jnp.where(ahead < 0, ahead + RING, ahead)
    far = ahead >= 16
    return 15 - 2 * m, jnp.where(far, ahead - 16, ahead), far


def spread_rows(factor):
    height, width = factor.shape
    return jnp.broadcast_to(factor[:, None, :], (height, TILE, width)).reshape(height * TILE, width)


def kernel(
    a_ref, b_ref, a_mask_ref, b_mask_ref, c_mask_ref, o_ref,
    a_in, b_in, a_marks, b_marks, c_marks, left, right, own, total, done, landed,
    in_sem, b_send, b_pass, b_recv, x_send, x_recv, a_send, a_recv, y_send, y_near, y_recv, k_send, k_recv, c_send, c_recv,
):
    row, col, zl = lax.axis_index("row"), lax.axis_index("col"), lax.axis_index("layer")
    x, zh = lax.rem(row, SIDE), row // SIDE
    y, core = col // 2, lax.rem(col, 2)
    z = zh * RUN + zl
    mine = mirrored(zl, zh)

    a_copy = pltpu.make_async_copy(a_ref, a_in, in_sem.at[0])
    b_copy = pltpu.make_async_copy(b_ref, b_in, in_sem.at[1])
    mask_copies = [
        pltpu.make_async_copy(source, held, in_sem.at[2 + number])
        for number, (source, held) in enumerate(
            ((a_mask_ref, a_marks), (b_mask_ref, b_marks), (c_mask_ref, c_marks))
        )
    ]
    for copy in (mask_copies[0], a_copy, mask_copies[1], b_copy, mask_copies[2]):
        copy.start()

    def at_z(there):
        return device(x, y, there, core)

    def at_x(step):
        return device(wrap(x + step, SIDE), y, z, core)

    def at_y(step):
        return device(x, wrap(y + step, SIDE), z, core)

    other = device(x, y, z, 1 - core)

    barrier = pltpu.get_barrier_semaphore()

    for high in range(RING // RUN):
        for low in range(RUN):
            @pl.when((zl != low) | (zh != high))
            def _():
                pl.semaphore_signal(barrier, inc=1, device_id=(high * SIDE + x, col, low), device_id_type=MESH)

    for step in range(1, SIDE):
        pl.semaphore_signal(barrier, inc=1, device_id=at_x(step), device_id_type=MESH)
        pl.semaphore_signal(barrier, inc=1, device_id=at_y(step), device_id_type=MESH)
    pl.semaphore_signal(barrier, inc=1, device_id=other, device_id_type=MESH)

    mask_copies[0].wait()
    spread = (
        lax.broadcasted_iota(jnp.int32, (NARROW // TILE, NARROW), 0)
        == lax.broadcasted_iota(jnp.int32, (NARROW // TILE, NARROW), 1) // TILE
    ).astype(F32)
    factor = lax.dot_general(
        a_marks[...].astype(F32), spread, (((0,), (0,)), ((), ())), preferred_element_type=F32
    )
    a_copy.wait()
    left[zl, core, y] = (a_in[...].astype(F32) * spread_rows(factor)).astype(BF16)

    width = b_ref.shape[1]
    tiles = width // TILE
    mask_copies[1].wait()
    marks = b_marks[...].astype(F32)
    spread = (
        lax.broadcasted_iota(jnp.int32, (tiles, width), 0) == lax.broadcasted_iota(jnp.int32, (tiles, width), 1) // TILE
    ).astype(F32)
    factor = spread_rows(jnp.dot(marks, spread, preferred_element_type=F32))
    b_copy.wait()
    for piece in range(RUN):
        for half in range(HALVES):
            cut = slice(piece * WIDE + half * HALF, piece * WIDE + (half + 1) * HALF)
            own[half, piece] = (b_in[:, cut].astype(F32) * factor[:, cut]).astype(BF16)
    for half in range(HALVES):
        right[half, mine, x, zh] = own[half, mine]

    pl.semaphore_wait(barrier, RING - 1 + 2 * (SIDE - 1) + 1)

    def a_hop(low, to):
        return pltpu.make_async_remote_copy(
            src_ref=left.at[low, core, y], dst_ref=left.at[low, core, y],
            send_sem=a_send.at[low, jnp.where(to > zl, 1, 0)], recv_sem=a_recv.at[low],
            device_id=device(x, y, zh * RUN + to, core), device_id_type=MESH,
        )

    way = jnp.where(core == 0, 1, SIDE - 1)
    back = SIDE - way

    def a_side(low, whose, step, near):
        there = wrap(y + whose, SIDE)
        return pltpu.make_async_remote_copy(
            src_ref=left.at[low, core, there], dst_ref=left.at[low, core, there],
            send_sem=y_send.at[low, 0 if near else jnp.where(whose == 0, 1, 2)],
            recv_sem=y_near.at[low] if near else y_recv.at[low],
            device_id=at_y(step), device_id_type=MESH,
        )

    def a_relay(low):
        view = left.at[low, core, wrap(y + back, SIDE)]
        pltpu.make_async_copy(view, view, y_near.at[low]).wait()
        a_side(low, back, way, False).start()

    def a_core(low):
        return pltpu.make_async_remote_copy(
            src_ref=left.at[low, core], dst_ref=left.at[low, core],
            send_sem=k_send.at[low], recv_sem=k_recv.at[low],
            device_id=other, device_id_type=MESH,
        )

    def a_onward(low):
        @pl.when((low <= zl) & (zl < RUN - 1))
        def _():
            a_hop(low, zl + 1).start()

        @pl.when((low >= zl) & (zl > 0))
        def _():
            a_hop(low, zl - 1).start()

        a_side(low, 0, way, True).start()
        a_side(low, 0, back, False).start()

    def a_arrive(low):
        pltpu.make_async_copy(left.at[low, core, y], left.at[low, core, y], a_recv.at[low]).wait()
        a_onward(low)

    def a_share(low):
        view = left.at[low, core, pl.ds(0, 2)]
        pltpu.make_async_copy(view, view, y_recv.at[low]).wait()
        a_core(low).start()

    def both_ways(step, act):
        @pl.when(zl - step >= 0)
        def _():
            act(zl - step)

        @pl.when(zl + step < RUN)
        def _():
            act(zl + step)

    def b_first(half, piece, to, way):
        return pltpu.make_async_remote_copy(
            src_ref=own.at[half, piece], dst_ref=right.at[half, mine, x, zh],
            send_sem=b_send.at[half, piece, way], recv_sem=b_recv.at[half, mine, zh],
            device_id=at_z(to), device_id_type=MESH,
        )

    def b_next(half, index, high, to):
        return pltpu.make_async_remote_copy(
            src_ref=right.at[half, index, x, high], dst_ref=right.at[half, index, x, high],
            send_sem=b_pass.at[half, index, high], recv_sem=b_recv.at[half, index, high],
            device_id=at_z(to), device_id_type=MESH,
        )

    def b_side(half, index, high, step):
        return pltpu.make_async_remote_copy(
            src_ref=right.at[half, index, x, high], dst_ref=right.at[half, index, x, high],
            send_sem=x_send.at[half, index, high, step - 1], recv_sem=x_recv.at[half, index],
            device_id=at_x(step), device_id_type=MESH,
        )

    def first_of(piece):
        gap, behind, _ = lap_of(z, piece)
        inside = behind <= gap
        up = jnp.where(inside, gap, 16) - behind
        down = behind - jnp.where(inside, 0, gap)
        return wrap(z + up, RING), up > 0, wrap(z - down + RING, RING), down > 0

    wide, behind_me, far_me = lap_of(z, mine)
    role = jnp.where(behind_me == 0, 0, 1) + jnp.where(far_me, 2, 0)
    narrow = 16 - wide

    def part(role):
        inside = jnp.where(role < 2, 1, 2), jnp.where(role == 0, -narrow, jnp.where(role == 1, narrow, 0))
        middle = (role == 1) | (role == 2)
        odd = (
            jnp.where(middle, 1, jnp.where(role == 3, 2, 3)),
            jnp.where(role == 2, wide, jnp.where(role == 3, narrow, 0)),
        )
        even = (
            jnp.where(middle, 1, jnp.where(role == 0, 2, 3)),
            jnp.where(role == 1, -wide, jnp.where(role == 0, -narrow, 0)),
        )
        return [64 * hops + 32 + step for hops, step in (inside, odd, even)]

    near_parts = part(role)
    far_parts = part(wrap(role + 2, 4))

    def route(index, high):
        low = mirrored(index, high)
        _, behind, far = lap_of(high * RUN + low, mine)
        near_code = jnp.where(behind <= wide, near_parts[0], jnp.where(lax.rem(low + mine, 2) == 1, near_parts[1], near_parts[2]))
        far_code = jnp.where(behind <= wide, far_parts[0], jnp.where(lax.rem(low + mine, 2) == 1, far_parts[1], far_parts[2]))
        code = jnp.where(far, far_code, near_code)
        step = lax.rem(code, 64) - 32
        return lax.div(code, 64), step != 0, lax.rem(z + step + RING, RING)

    def group_of(stage):
        half = stage // RUN
        return half, wrap(mine - (stage - half * RUN) + RUN, RUN)

    def b_launch(stage):
        half = stage // RUN
        piece = wrap(mine + stage - half * RUN, RUN)
        to_up, up, to_down, down = first_of(piece)

        @pl.when(up)
        def _():
            b_first(half, piece, to_up, 1).start()

        @pl.when(down)
        def _():
            b_first(half, piece, to_down, 0).start()

    def b_handle(stage, hops_now):
        half, index = group_of(stage)
        for high in range(RING // RUN):
            hops, onward, to = route(index, high)

            @pl.when(hops == hops_now)
            def _():
                @pl.when((index != mine) | (high != zh))
                def _():
                    view = right.at[half, index, x, high]
                    pltpu.make_async_copy(view, view, b_recv.at[half, index, high]).wait()

                @pl.when(onward)
                def _():
                    b_next(half, index, high, to).start()

                for side in (1, 3, 2):
                    b_side(half, index, high, side).start()

    def use(stage):
        half, index = group_of(stage)
        view = right.at[half, index, pl.ds(0, SIDE - 1)]
        pltpu.make_async_copy(view, view, x_recv.at[half, index]).wait()
        lows = [index if high % 2 == 0 else RUN - 1 - index for high in range(RING // RUN)]
        blocks = [left[lows[high], c, high] for high in range(SIDE) for c in range(2)]
        depths = [right[half, index, s, high] for high in range(RING // RUN) for s in range(SIDE)]
        total[half] += jnp.dot(
            jnp.concatenate(blocks, axis=1), jnp.concatenate(depths, axis=0), preferred_element_type=F32
        )

    def c_out(half, low):
        return pltpu.make_async_remote_copy(
            src_ref=done.at[half, low], dst_ref=landed.at[half, mine],
            send_sem=c_send.at[half, low], recv_sem=c_recv.at[half],
            device_id=device(x, y, zh * RUN + low, core), device_id_type=MESH,
        )

    def finish(half):
        keep = (
            lax.broadcasted_iota(jnp.int32, (tiles, HALF), 0)
            == lax.broadcasted_iota(jnp.int32, (tiles, HALF), 1) // TILE + mine * (WIDE // TILE) + half * (HALF // TILE)
        ).astype(F32)
        factor = jnp.dot(c_marks[...].astype(F32), keep, preferred_element_type=F32)
        done[half] = (total[half] * spread_rows(factor)).astype(BF16).reshape(RUN, ROWS // RUN, HALF)

        @pl.loop(1, RUN)
        def _(step):
            c_out(half, wrap(zl + step, RUN)).start()

        landed[half, mine] = done[half, zl]

    a_onward(zl)
    total[...] = jnp.zeros_like(total)
    mask_copies[2].wait()

    @pl.loop(0, RUN)
    def _(stage):
        b_launch(stage)

    last = max(RUN + 1, RUN // GPS + LAG3)

    def staged(step, act):
        for turn in range(GPS):
            stage = step * GPS + turn

            @pl.when((stage >= 0) & (stage < RUN))
            def _():
                act(stage)

    @pl.loop(0, last)
    def _(step):
        @pl.when(step < RUN - 1)
        def _():
            both_ways(step + 1, a_arrive)

        @pl.when(step == 0)
        def _():
            a_relay(zl)

        @pl.when((step > 0) & (step < RUN))
        def _():
            both_ways(step, a_relay)

        staged(step, lambda stage: b_handle(stage, 1))
        staged(step - LAG2, lambda stage: b_handle(stage, 2))
        staged(step - LAG3, lambda stage: b_handle(stage, 3))

        @pl.when((step >= 1) & (step < RUN + 1))
        def _():
            @pl.when(step == 1)
            def _():
                a_share(zl)

            @pl.when(step > 1)
            def _():
                both_ways(step - 1, a_share)

    @pl.loop(0, RUN)
    def _(low):
        pltpu.make_async_copy(left.at[low, core], left.at[low, core], k_recv.at[low]).wait()

    @pl.loop(0, RUN)
    def _(stage):
        use(stage)

    finish(HALVES - 1)

    @pl.loop(0, RUN)
    def _(index):
        @pl.when((index <= zl) & (zl < RUN - 1))
        def _():
            a_hop(index, zl + 1).wait_send()

        @pl.when((index >= zl) & (zl > 0))
        def _():
            a_hop(index, zl - 1).wait_send()

        a_side(index, 0, way, True).wait_send()
        a_side(index, 0, back, False).wait_send()
        a_side(index, back, way, False).wait_send()
        a_core(index).wait_send()

        to_up, up, to_down, down = first_of(index)
        for half in range(HALVES):
            @pl.when(up)
            def _():
                b_first(half, index, to_up, 1).wait_send()

            @pl.when(down)
            def _():
                b_first(half, index, to_down, 0).wait_send()

            for high in range(RING // RUN):
                for step in (1, 2, 3):
                    b_side(half, index, high, step).wait_send()

        for high in range(RING // RUN):
            _, onward, to = route(index, high)

            @pl.when(onward)
            def _():
                for half in range(HALVES):
                    b_next(half, index, high, to).wait_send()

    for half in range(HALVES):
        view = landed.at[half, pl.ds(0, RUN - 1)]
        pltpu.make_async_copy(view, view, c_recv.at[half]).wait()
        for piece in range(RUN):
            cut = slice(piece * WIDE + half * HALF, piece * WIDE + (half + 1) * HALF)
            o_ref[:, cut] = landed[half, piece]

    @pl.loop(0, RUN)
    def _(index):
        @pl.when(index != zl)
        def _():
            for half in range(HALVES):
                c_out(half, index).wait_send()


def body(a_tiles, b_tiles, a_mask, b_mask, c_mask):
    width = b_tiles.shape[2]
    dma = pltpu.SemaphoreType.DMA
    runs = RING // RUN
    return pl.pallas_call(
        kernel,
        out_shape=jax.ShapeDtypeStruct((ROWS // RUN, width), BF16),
        in_specs=[pl.BlockSpec(memory_space=pltpu.HBM)] * 5,
        out_specs=pl.BlockSpec(memory_space=pltpu.VMEM),
        scratch_shapes=[
            pltpu.VMEM((ROWS, NARROW), BF16),
            pltpu.VMEM((DEEP, width), BF16),
            pltpu.VMEM((NARROW // TILE, ROWS // TILE), jnp.int32),
            pltpu.VMEM((DEEP // TILE, width // TILE), jnp.int32),
            pltpu.VMEM((ROWS // TILE, width // TILE), jnp.int32),
            pltpu.VMEM((RUN, 2, SIDE, ROWS, NARROW), BF16),
            pltpu.VMEM((HALVES, RUN, SIDE, runs, DEEP, HALF), BF16),
            pltpu.VMEM((HALVES, RUN, DEEP, HALF), BF16),
            pltpu.VMEM((HALVES, ROWS, HALF), F32),
            pltpu.VMEM((HALVES, RUN, ROWS // RUN, HALF), BF16),
            pltpu.VMEM((HALVES, RUN, ROWS // RUN, HALF), BF16),
            dma((5,)),
            dma((HALVES, RUN, 2)), dma((HALVES, RUN, runs)), dma((HALVES, RUN, runs)),
            dma((HALVES, RUN, runs, SIDE - 1)), dma((HALVES, RUN)),
            dma((RUN, 2)), dma((RUN,)),
            dma((RUN, SIDE - 1)), dma((RUN,)), dma((RUN,)),
            dma((RUN,)), dma((RUN,)),
            dma((HALVES, RUN)), dma((HALVES,)),
        ],
        compiler_params=pltpu.CompilerParams(
            collective_id=0, has_side_effects=True, vmem_limit_bytes=63 << 20
        ),
        cost_estimate=pl.CostEstimate(
            flops=2 * ROWS * WIDE * 8192, bytes_accessed=1 << 20, transcendentals=0
        ),
        name="purify",
    )(a_tiles[0], b_tiles[0], a_mask[0].T, b_mask[0], c_mask)


def solution(mesh):
    placed = (
        P("layer", "row", "col"),
        P("layer", "row", "col"),
        P("layer", "row", "col"),
        P("layer", "row", "col"),
        P("row", "col"),
    )
    return jax.shard_map(
        body, mesh=mesh, in_specs=placed, out_specs=P(("row", "layer"), "col"), check_vma=False
    )
```

```python
import jax
import jax.numpy as jnp
from jax import lax
from jax.experimental import pallas as pl
from jax.experimental.pallas import tpu as pltpu
from jax.sharding import PartitionSpec as P

TILE = 32
RUN = 8
RING = 32
SIDE = 4
WIDE = 256
DEEP = 64
ROWS = 512
NARROW = 128
HALVES = 1
HALF = WIDE // HALVES
GPS = 2
LAG2 = 3
LAG3 = 4
MESH = pl.DeviceIdType.MESH
F32 = jnp.float32
BF16 = jnp.bfloat16


def device(x, y, z, core):
    return (lax.div(z, RUN) * SIDE + x, y * 2 + core, lax.rem(z, RUN))


def wrap(number, size):
    return jnp.where(number >= size, number - size, number)


def mirrored(index, high):
    return jnp.where(high % 2 == 0, index, RUN - 1 - index)


def lap_of(source, piece):
    early = piece < RUN // 2
    m = jnp.where(early, piece, RUN - 1 - piece)
    ahead = source - jnp.where(early, m, m + RUN)
    ahead = jnp.where(ahead < 0, ahead + RING, ahead)
    far = ahead >= 16
    return 15 - 2 * m, jnp.where(far, ahead - 16, ahead), far


def spread_rows(factor):
    height, width = factor.shape
    return jnp.broadcast_to(factor[:, None, :], (height, TILE, width)).reshape(height * TILE, width)


def kernel(
    a_ref, b_ref, a_mask_ref, b_mask_ref, c_mask_ref, o_ref,
    a_in, b_in, a_marks, b_marks, c_marks, left, right, own, total, done, landed,
    in_sem, b_send, b_pass, b_recv, x_send, x_recv, a_send, a_recv, y_send, y_near, y_recv, k_send, k_recv, c_send, c_recv,
):
    row, col, zl = lax.axis_index("row"), lax.axis_index("col"), lax.axis_index("layer")
    x, zh = lax.rem(row, SIDE), row // SIDE
    y, core = col // 2, lax.rem(col, 2)
    z = zh * RUN + zl
    mine = mirrored(zl, zh)

    a_copy = pltpu.make_async_copy(a_ref, a_in, in_sem.at[0])
    b_copy = pltpu.make_async_copy(b_ref, b_in, in_sem.at[1])
    mask_copies = [
        pltpu.make_async_copy(source, held, in_sem.at[2 + number])
        for number, (source, held) in enumerate(
            ((a_mask_ref, a_marks), (b_mask_ref, b_marks), (c_mask_ref, c_marks))
        )
    ]
    for copy in (mask_copies[0], a_copy, mask_copies[1], b_copy, mask_copies[2]):
        copy.start()

    def at_z(there):
        return device(x, y, there, core)

    def at_x(step):
        return device(wrap(x + step, SIDE), y, z, core)

    def at_y(step):
        return device(x, wrap(y + step, SIDE), z, core)

    other = device(x, y, z, 1 - core)

    barrier = pltpu.get_barrier_semaphore()

    for high in range(RING // RUN):
        for low in range(RUN):
            @pl.when((zl != low) | (zh != high))
            def _():
                pl.semaphore_signal(barrier, inc=1, device_id=(high * SIDE + x, col, low), device_id_type=MESH)

    for step in range(1, SIDE):
        pl.semaphore_signal(barrier, inc=1, device_id=at_x(step), device_id_type=MESH)
        pl.semaphore_signal(barrier, inc=1, device_id=at_y(step), device_id_type=MESH)
    pl.semaphore_signal(barrier, inc=1, device_id=other, device_id_type=MESH)

    mask_copies[0].wait()
    spread = (
        lax.broadcasted_iota(jnp.int32, (NARROW // TILE, NARROW), 0)
        == lax.broadcasted_iota(jnp.int32, (NARROW // TILE, NARROW), 1) // TILE
    ).astype(F32)
    factor = lax.dot_general(
        a_marks[...].astype(F32), spread, (((0,), (0,)), ((), ())), preferred_element_type=F32
    )
    a_copy.wait()
    left[zl, core, y] = (a_in[...].astype(F32) * spread_rows(factor)).astype(BF16)

    pl.semaphore_wait(barrier, RING - 1 + 2 * (SIDE - 1) + 1)

    def a_hop(low, to):
        return pltpu.make_async_remote_copy(
            src_ref=left.at[low, core, y], dst_ref=left.at[low, core, y],
            send_sem=a_send.at[low, jnp.where(to > zl, 1, 0)], recv_sem=a_recv.at[low],
            device_id=device(x, y, zh * RUN + to, core), device_id_type=MESH,
        )

    way = jnp.where(core == 0, 1, SIDE - 1)
    back = SIDE - way

    def a_side(low, whose, step, near):
        there = wrap(y + whose, SIDE)
        return pltpu.make_async_remote_copy(
            src_ref=left.at[low, core, there], dst_ref=left.at[low, core, there],
            send_sem=y_send.at[low, 0 if near else jnp.where(whose == 0, 1, 2)],
            recv_sem=y_near.at[low] if near else y_recv.at[low],
            device_id=at_y(step), device_id_type=MESH,
        )

    def a_relay(low):
        view = left.at[low, core, wrap(y + back, SIDE)]
        pltpu.make_async_copy(view, view, y_near.at[low]).wait()
        a_side(low, back, way, False).start()

    def a_core(low):
        return pltpu.make_async_remote_copy(
            src_ref=left.at[low, core], dst_ref=left.at[low, core],
            send_sem=k_send.at[low], recv_sem=k_recv.at[low],
            device_id=other, device_id_type=MESH,
        )

    def a_onward(low):
        @pl.when((low <= zl) & (zl < RUN - 1))
        def _():
            a_hop(low, zl + 1).start()

        @pl.when((low >= zl) & (zl > 0))
        def _():
            a_hop(low, zl - 1).start()

        a_side(low, 0, way, True).start()
        a_side(low, 0, back, False).start()

    def a_arrive(low):
        pltpu.make_async_copy(left.at[low, core, y], left.at[low, core, y], a_recv.at[low]).wait()
        a_onward(low)

    def a_share(low):
        view = left.at[low, core, pl.ds(0, 2)]
        pltpu.make_async_copy(view, view, y_recv.at[low]).wait()
        a_core(low).start()

    def both_ways(step, act):
        @pl.when(zl - step >= 0)
        def _():
            act(zl - step)

        @pl.when(zl + step < RUN)
        def _():
            act(zl + step)

    def b_first(half, piece, to, way):
        return pltpu.make_async_remote_copy(
            src_ref=own.at[half, piece], dst_ref=right.at[half, mine, x, zh],
            send_sem=b_send.at[half, piece, way], recv_sem=b_recv.at[half, mine, zh],
            device_id=at_z(to), device_id_type=MESH,
        )

    def b_next(half, index, high, to):
        return pltpu.make_async_remote_copy(
            src_ref=right.at[half, index, x, high], dst_ref=right.at[half, index, x, high],
            send_sem=b_pass.at[half, index, high], recv_sem=b_recv.at[half, index, high],
            device_id=at_z(to), device_id_type=MESH,
        )

    def b_side(half, index, high, step):
        return pltpu.make_async_remote_copy(
            src_ref=right.at[half, index, x, high], dst_ref=right.at[half, index, x, high],
            send_sem=x_send.at[half, index, high, step - 1], recv_sem=x_recv.at[half, index],
            device_id=at_x(step), device_id_type=MESH,
        )

    def first_of(piece):
        gap, behind, _ = lap_of(z, piece)
        inside = behind <= gap
        up = jnp.where(inside, gap, 16) - behind
        down = behind - jnp.where(inside, 0, gap)
        return wrap(z + up, RING), up > 0, wrap(z - down + RING, RING), down > 0

    wide, behind_me, far_me = lap_of(z, mine)
    role = jnp.where(behind_me == 0, 0, 1) + jnp.where(far_me, 2, 0)
    narrow = 16 - wide

    def part(role):
        inside = jnp.where(role < 2, 1, 2), jnp.where(role == 0, -narrow, jnp.where(role == 1, narrow, 0))
        middle = (role == 1) | (role == 2)
        odd = (
            jnp.where(middle, 1, jnp.where(role == 3, 2, 3)),
            jnp.where(role == 2, wide, jnp.where(role == 3, narrow, 0)),
        )
        even = (
            jnp.where(middle, 1, jnp.where(role == 0, 2, 3)),
            jnp.where(role == 1, -wide, jnp.where(role == 0, -narrow, 0)),
        )
        return [64 * hops + 32 + step for hops, step in (inside, odd, even)]

    near_parts = part(role)
    far_parts = part(wrap(role + 2, 4))

    def route(index, high):
        low = mirrored(index, high)
        _, behind, far = lap_of(high * RUN + low, mine)
        near_code = jnp.where(behind <= wide, near_parts[0], jnp.where(lax.rem(low + mine, 2) == 1, near_parts[1], near_parts[2]))
        far_code = jnp.where(behind <= wide, far_parts[0], jnp.where(lax.rem(low + mine, 2) == 1, far_parts[1], far_parts[2]))
        code = jnp.where(far, far_code, near_code)
        step = lax.rem(code, 64) - 32
        return lax.div(code, 64), step != 0, lax.rem(z + step + RING, RING)

    def group_of(stage):
        half = stage // RUN
        return half, wrap(mine - (stage - half * RUN) + RUN, RUN)

    def b_launch(stage):
        half = stage // RUN
        piece = wrap(mine + stage - half * RUN, RUN)
        to_up, up, to_down, down = first_of(piece)

        @pl.when(up)
        def _():
            b_first(half, piece, to_up, 1).start()

        @pl.when(down)
        def _():
            b_first(half, piece, to_down, 0).start()

    def b_handle(stage, hops_now):
        half, index = group_of(stage)
        for high in range(RING // RUN):
            hops, onward, to = route(index, high)

            @pl.when(hops == hops_now)
            def _():
                @pl.when((index != mine) | (high != zh))
                def _():
                    view = right.at[half, index, x, high]
                    pltpu.make_async_copy(view, view, b_recv.at[half, index, high]).wait()

                @pl.when(onward)
                def _():
                    b_next(half, index, high, to).start()

                for side in (1, 3, 2):
                    b_side(half, index, high, side).start()

    def use(stage):
        half, index = group_of(stage)
        view = right.at[half, index, pl.ds(0, SIDE - 1)]
        pltpu.make_async_copy(view, view, x_recv.at[half, index]).wait()
        lows = [index if high % 2 == 0 else RUN - 1 - index for high in range(RING // RUN)]
        blocks = [left[lows[high], c, high] for high in range(SIDE) for c in range(2)]
        depths = [right[half, index, s, high] for high in range(RING // RUN) for s in range(SIDE)]
        total[half] += jnp.dot(
            jnp.concatenate(blocks, axis=1), jnp.concatenate(depths, axis=0), preferred_element_type=F32
        )

    def c_out(half, low):
        return pltpu.make_async_remote_copy(
            src_ref=done.at[half, low], dst_ref=landed.at[half, mine],
            send_sem=c_send.at[half, low], recv_sem=c_recv.at[half],
            device_id=device(x, y, zh * RUN + low, core), device_id_type=MESH,
        )

    def finish(half):
        keep = (
            lax.broadcasted_iota(jnp.int32, (tiles, HALF), 0)
            == lax.broadcasted_iota(jnp.int32, (tiles, HALF), 1) // TILE + mine * (WIDE // TILE) + half * (HALF // TILE)
        ).astype(F32)
        factor = jnp.dot(c_marks[...].astype(F32), keep, preferred_element_type=F32)
        done[half] = (total[half] * spread_rows(factor)).astype(BF16).reshape(RUN, ROWS // RUN, HALF)

        @pl.loop(1, RUN)
        def _(step):
            c_out(half, wrap(zl + step, RUN)).start()

        landed[half, mine] = done[half, zl]

    a_onward(zl)

    width = b_ref.shape[1]
    tiles = width // TILE
    mask_copies[1].wait()
    marks = b_marks[...].astype(F32)
    spread = (
        lax.broadcasted_iota(jnp.int32, (tiles, width), 0) == lax.broadcasted_iota(jnp.int32, (tiles, width), 1) // TILE
    ).astype(F32)
    factor = spread_rows(jnp.dot(marks, spread, preferred_element_type=F32))
    b_copy.wait()
    for piece in range(RUN):
        for half in range(HALVES):
            cut = slice(piece * WIDE + half * HALF, piece * WIDE + (half + 1) * HALF)
            own[half, piece] = (b_in[:, cut].astype(F32) * factor[:, cut]).astype(BF16)
    for half in range(HALVES):
        right[half, mine, x, zh] = own[half, mine]
    total[...] = jnp.zeros_like(total)
    mask_copies[2].wait()

    @pl.loop(0, RUN)
    def _(stage):
        b_launch(stage)

    last = max(RUN + 1, RUN // GPS + LAG3)

    def staged(step, act):
        for turn in range(GPS):
            stage = step * GPS + turn

            @pl.when((stage >= 0) & (stage < RUN))
            def _():
                act(stage)

    @pl.loop(0, last)
    def _(step):
        @pl.when(step < RUN - 1)
        def _():
            both_ways(step + 1, a_arrive)

        @pl.when(step == 0)
        def _():
            a_relay(zl)

        @pl.when((step > 0) & (step < RUN))
        def _():
            both_ways(step, a_relay)

        staged(step, lambda stage: b_handle(stage, 1))
        staged(step - LAG2, lambda stage: b_handle(stage, 2))
        staged(step - LAG3, lambda stage: b_handle(stage, 3))

        @pl.when((step >= 1) & (step < RUN + 1))
        def _():
            @pl.when(step == 1)
            def _():
                a_share(zl)

            @pl.when(step > 1)
            def _():
                both_ways(step - 1, a_share)

    @pl.loop(0, RUN)
    def _(low):
        pltpu.make_async_copy(left.at[low, core], left.at[low, core], k_recv.at[low]).wait()

    @pl.loop(0, RUN)
    def _(stage):
        use(stage)

    finish(HALVES - 1)

    @pl.loop(0, RUN)
    def _(index):
        @pl.when((index <= zl) & (zl < RUN - 1))
        def _():
            a_hop(index, zl + 1).wait_send()

        @pl.when((index >= zl) & (zl > 0))
        def _():
            a_hop(index, zl - 1).wait_send()

        a_side(index, 0, way, True).wait_send()
        a_side(index, 0, back, False).wait_send()
        a_side(index, back, way, False).wait_send()
        a_core(index).wait_send()

        to_up, up, to_down, down = first_of(index)
        for half in range(HALVES):
            @pl.when(up)
            def _():
                b_first(half, index, to_up, 1).wait_send()

            @pl.when(down)
            def _():
                b_first(half, index, to_down, 0).wait_send()

            for high in range(RING // RUN):
                for step in (1, 2, 3):
                    b_side(half, index, high, step).wait_send()

        for high in range(RING // RUN):
            _, onward, to = route(index, high)

            @pl.when(onward)
            def _():
                for half in range(HALVES):
                    b_next(half, index, high, to).wait_send()

    for half in range(HALVES):
        view = landed.at[half, pl.ds(0, RUN - 1)]
        pltpu.make_async_copy(view, view, c_recv.at[half]).wait()
        for piece in range(RUN):
            cut = slice(piece * WIDE + half * HALF, piece * WIDE + (half + 1) * HALF)
            o_ref[:, cut] = landed[half, piece]

    @pl.loop(0, RUN)
    def _(index):
        @pl.when(index != zl)
        def _():
            for half in range(HALVES):
                c_out(half, index).wait_send()


def body(a_tiles, b_tiles, a_mask, b_mask, c_mask):
    width = b_tiles.shape[2]
    dma = pltpu.SemaphoreType.DMA
    runs = RING // RUN
    return pl.pallas_call(
        kernel,
        out_shape=jax.ShapeDtypeStruct((ROWS // RUN, width), BF16),
        in_specs=[pl.BlockSpec(memory_space=pltpu.HBM)] * 5,
        out_specs=pl.BlockSpec(memory_space=pltpu.VMEM),
        scratch_shapes=[
            pltpu.VMEM((ROWS, NARROW), BF16),
            pltpu.VMEM((DEEP, width), BF16),
            pltpu.VMEM((NARROW // TILE, ROWS // TILE), jnp.int32),
            pltpu.VMEM((DEEP // TILE, width // TILE), jnp.int32),
            pltpu.VMEM((ROWS // TILE, width // TILE), jnp.int32),
            pltpu.VMEM((RUN, 2, SIDE, ROWS, NARROW), BF16),
            pltpu.VMEM((HALVES, RUN, SIDE, runs, DEEP, HALF), BF16),
            pltpu.VMEM((HALVES, RUN, DEEP, HALF), BF16),
            pltpu.VMEM((HALVES, ROWS, HALF), F32),
            pltpu.VMEM((HALVES, RUN, ROWS // RUN, HALF), BF16),
            pltpu.VMEM((HALVES, RUN, ROWS // RUN, HALF), BF16),
            dma((5,)),
            dma((HALVES, RUN, 2)), dma((HALVES, RUN, runs)), dma((HALVES, RUN, runs)),
            dma((HALVES, RUN, runs, SIDE - 1)), dma((HALVES, RUN)),
            dma((RUN, 2)), dma((RUN,)),
            dma((RUN, SIDE - 1)), dma((RUN,)), dma((RUN,)),
            dma((RUN,)), dma((RUN,)),
            dma((HALVES, RUN)), dma((HALVES,)),
        ],
        compiler_params=pltpu.CompilerParams(
            collective_id=0, has_side_effects=True, vmem_limit_bytes=63 << 20
        ),
        cost_estimate=pl.CostEstimate(
            flops=2 * ROWS * WIDE * 8192, bytes_accessed=1 << 20, transcendentals=0
        ),
        name="purify",
    )(a_tiles[0], b_tiles[0], a_mask[0].T, b_mask[0], c_mask)


def solution(mesh):
    placed = (
        P("layer", "row", "col"),
        P("layer", "row", "col"),
        P("layer", "row", "col"),
        P("layer", "row", "col"),
        P("row", "col"),
    )
    return jax.shard_map(
        body, mesh=mesh, in_specs=placed, out_specs=P(("row", "layer"), "col"), check_vma=False
    )
```
